32 devices in a mesh: groups: 2 (over y), bucket: 4 (over z), rel: 2 (over x), sub: 2 (over core).
Axes of the slice: x: 2, y: 2, z: 4, core: 2. Of those that a mesh axis runs over, the one named last changes fastest.
Arguments:
- entity: float32 [2048, 256], P(('groups', 'bucket')), parts along dimension 0, may hold values from -2.5 to 2.5
- entity_acc: float32 [2048], P(('groups', 'bucket')), parts along dimension 0, may hold values from 0.01 to 1
- relation: float32 [2048, 256], P(('groups', 'rel')), parts along dimension 0, may hold values from -4 to 4
- relation_acc: float32 [2048], P(('groups', 'rel')), parts along dimension 0, may hold values from 0.01 to 1
- edge_src: int32 [8, 2, 1, 1024], P(('groups', 'bucket'), 'rel'), parts along dimension 0, may hold values from 0 to 255
- edge_dst: int32 [8, 2, 1, 1024], P(('groups', 'bucket'), 'rel'), parts along dimension 0, may hold values from 0 to 255
- edge_rel: int32 [8, 2, 1, 1024], P(('groups', 'bucket'), 'rel'), parts along dimension 0, may hold values from 0 to 511
- negatives: int32 [8, 2, 1, 1024], P(('groups', 'bucket'), 'rel', None, 'sub'), parts along dimension 0, may hold values from 0 to 255
- ovf_src: int32 [8, 2, 2, 8, 128], P(('groups', 'bucket'), 'rel', 'sub'), parts along dimension 0, may hold values from 0 to 255
- ovf_dst: int32 [8, 2, 2, 8, 128], P(('groups', 'bucket'), 'rel', 'sub'), parts along dimension 0, may hold values from 0 to 255
- ovf_rel: int32 [8, 2, 2, 8, 128], P(('groups', 'bucket'), 'rel', 'sub'), parts along dimension 0, may hold values from 0 to 511
- ovf_count: int32 [4, 2, 4], P(('groups', 'rel'), 'sub'), parts along dimension 0, may hold values from 1 to 8, 16 in all within a row
Outputs:
- new_entity: float32 [2048, 256], P(('groups', 'bucket')), parts along dimension 0
- new_entity_acc: float32 [2048], P(('groups', 'bucket')), parts along dimension 0
- new_relation: float32 [2048, 256], P(('groups', 'rel')), parts along dimension 0
- new_relation_acc: float32 [2048], P(('groups', 'rel')), parts along dimension 0
The draws below stay inside these ranges and needn't reach their ends.
There are 2 independent parts, one for each index of `groups`. The reference program is written for one: setup_inputs(seed, part) draws one part's arguments, and reference() takes and returns one part's arrays. A program takes and returns all parts, laid end to end along the dimension named above; each array names one. Nothing has to cross between parts.
Inputs may be any that keep to these rules, and one draw needn't show every extreme that they name: `ovf_count`: for each relation group and sub index, the counts over the 4 buckets sum to 16, and the largest of them is 8.
All inputs are finite; a program needn't handle non-finite values.
Results may differ from the reference program's by a relative error of at most 0.0001.
Values sent between devices are 32-bit elements; how exact they have to be, the bound alone decides.
A program may use at most 64 MiB of HBM per device.

```python
import math
import jax
import jax.numpy as jnp
import numpy as np
from jax import lax

D = 256
ENT_DEV = 256
REL_DEV = 512
BLOCKS = 1
CH = 1024
NEG = 1024
OCH = 128
OVF = 8
ENTITIES = 1024
RELS = 1024
N_BUCKET = 4
N_REL = 2
N_SUB = 2


def set_ends(entries, key, low, high):
    index_at = [jax.random.randint(jax.random.fold_in(key, axis), (), 0, length) for axis, length in enumerate(entries.shape)]
    main_axis = entries.shape.index(max(entries.shape))
    neighbour = index_at[:main_axis] + [(index_at[main_axis] + 1) % entries.shape[main_axis]] + index_at[main_axis + 1:]
    return entries.at[tuple(index_at)].set(low).at[tuple(neighbour)].set(high)


def shard_levels(key, dims, pieces, least, high):
    def one(position, shards_of):
        heights = jax.random.uniform(jax.random.fold_in(jax.random.fold_in(key, 6), position), (shards_of,), jnp.float32, least / len(pieces), high / len(pieces))
        return jnp.repeat(jnp.exp(heights), dims[position] // shards_of).reshape((-1,) + (1,) * (len(dims) - position - 1))

    level = one(*pieces[0])
    for cut in pieces[1:]:
        level = level * one(*cut)
    return level


def length_profile(number_of, total, reach, lean):
    weights = [(1 << 20) // math.isqrt(standing ** lean) + 1 for standing in range(2, number_of + 1)]
    surplus, given = total - reach - (number_of - 1), [1] * (number_of - 1)
    while surplus > 0:
        candidates = [i for i in range(number_of - 1) if given[i] < reach]
        whole, remaining = sum([weights[i] for i in candidates]), surplus
        for i in candidates:
            more = min(reach - given[i], max(1, remaining * weights[i] // whole), surplus)
            given[i] = given[i] + more
            surplus = surplus - more
    return np.array([reach] + given)


def ragged(key, count, total, limit, lean):
    if count == 2:
        one = jax.random.randint(key, (), max(1, total - limit), min(limit, total - 1) + 1)
        return jnp.stack([one, total - one])
    lengths = jnp.asarray(length_profile(count, total, limit, lean), jnp.int32)
    couples = (count - 1) // 2
    source_of, receiver = lengths[1:1 + 2 * couples:2], lengths[2:2 + 2 * couples:2]
    margin = jnp.minimum(source_of - 1, limit - receiver)
    shifted = jax.random.randint(jax.random.fold_in(key, 1), (couples,), 0, 1 << 20) % (margin + 1)
    lengths = lengths.at[1:1 + 2 * couples:2].set(source_of - shifted).at[2:2 + 2 * couples:2].set(receiver + shifted)
    return lengths[jax.random.permutation(jax.random.fold_in(key, 2), count)]


def centred(rng, extent, width, limit, shards=(), kind=jnp.bfloat16):
    entries = jax.random.normal(rng, extent, jnp.float32) * width
    if len(shards) > 0:
        entries = shard_levels(rng, extent, shards, -0.22, 0.18) * entries
    return jnp.clip(entries, min=-limit, max=limit).astype(kind)


def setup_inputs(seed: int = 0, part: int = 0) -> dict:
    key_of = jax.random.split(jax.random.key(seed), 13)
    part_keys = jax.random.split(jax.random.fold_in(key_of[12], part), 13)
    return {
        "entity": centred(part_keys[0], (ENTITIES, D), 0.35, 2.5, ((0, 4),), jnp.float32),
        "entity_acc": jnp.clip(jnp.exp(math.log(1.0) - 4.6051702 * jax.random.uniform(part_keys[1], (ENTITIES,), jnp.float32) ** shard_levels(part_keys[1], (ENTITIES,), ((0, 4),), -0.2, 0.2)), 0.01, 1.0),
        "relation": centred(part_keys[2], (RELS, D), 1.0, 4.0, ((0, 2),), jnp.float32),
        "relation_acc": jnp.clip(jnp.exp(math.log(1.0) - 4.6051702 * jax.random.uniform(part_keys[3], (RELS,), jnp.float32) ** shard_levels(part_keys[3], (RELS,), ((0, 2),), -0.2, 0.2)), 0.01, 1.0),
        "edge_src": set_ends(jax.random.randint(part_keys[4], (N_BUCKET, N_REL, BLOCKS, CH), 0, ENT_DEV), jax.random.fold_in(part_keys[4], 1), 0, ENT_DEV - 1).astype(jnp.int32),
        "edge_dst": set_ends(jax.random.randint(part_keys[5], (N_BUCKET, N_REL, BLOCKS, CH), 0, ENT_DEV), jax.random.fold_in(part_keys[5], 1), 0, ENT_DEV - 1).astype(jnp.int32),
        "edge_rel": set_ends(jax.random.randint(part_keys[6], (N_BUCKET, N_REL, BLOCKS, CH), 0, REL_DEV), jax.random.fold_in(part_keys[6], 1), 0, REL_DEV - 1).astype(jnp.int32),
        "negatives": set_ends(jax.random.randint(part_keys[7], (N_BUCKET, N_REL, BLOCKS, NEG), 0, ENT_DEV), jax.random.fold_in(part_keys[7], 1), 0, ENT_DEV - 1).astype(jnp.int32),
        "ovf_src": set_ends(jax.random.randint(part_keys[8], (N_BUCKET, N_REL, N_SUB, OVF, OCH), 0, ENT_DEV), jax.random.fold_in(part_keys[8], 1), 0, ENT_DEV - 1).astype(jnp.int32),
        "ovf_dst": set_ends(jax.random.randint(part_keys[9], (N_BUCKET, N_REL, N_SUB, OVF, OCH), 0, ENT_DEV), jax.random.fold_in(part_keys[9], 1), 0, ENT_DEV - 1).astype(jnp.int32),
        "ovf_rel": set_ends(jax.random.randint(part_keys[10], (N_BUCKET, N_REL, N_SUB, OVF, OCH), 0, REL_DEV), jax.random.fold_in(part_keys[10], 1), 0, REL_DEV - 1).astype(jnp.int32),
        "ovf_count": jax.vmap(lambda own: ragged(own, N_BUCKET, N_BUCKET * OVF // 2, OVF, 2))(jax.random.split(part_keys[11], N_REL * N_SUB)).reshape((N_REL, N_SUB, N_BUCKET)).astype(jnp.int32),
    }


HI = lax.Precision.HIGHEST

def block_grads(q, dst_rows, neg_rows, pos_weight):
    pos = lax.optimization_barrier(jnp.sum(q * dst_rows, axis=-1))
    scores = jnp.dot(q, neg_rows.T, precision=HI)
    dpos = -jax.nn.sigmoid(-pos) * pos_weight
    dneg = jax.nn.sigmoid(scores) * (1.0 / NEG)
    dq = dpos[:, None] * dst_rows + jnp.dot(dneg, neg_rows, precision=HI)
    ddst = dpos[:, None] * q
    dnegrows = jnp.dot(dneg.T, q, precision=HI)
    return (dq, ddst, dnegrows)

def spill_grads(queries, dests, live):
    scores = jnp.einsum('mid,mkd->mik', queries, dests, precision=HI)
    pos = lax.optimization_barrier(jnp.sum(queries * dests, axis=-1))
    ident = jnp.eye(OCH, dtype=jnp.float32)
    dscore = jax.nn.sigmoid(scores) * (1.0 / OCH) + ident[None] * (-jax.nn.sigmoid(-pos))[:, :, None]
    dscore = dscore * live[:, None, None]
    dq = jnp.einsum('mik,mkd->mid', dscore, dests, precision=HI)
    ddst = jnp.einsum('mik,mid->mkd', dscore, queries, precision=HI)
    return (dq, ddst)

def adagrad(table, accum, grad):
    fresh = accum + lax.optimization_barrier(jnp.mean(grad * grad, axis=-1))
    return (table - 0.1 * grad / jnp.sqrt(fresh)[:, None], fresh)

def reference(entity, entity_acc, relation, relation_acc, edge_src, edge_dst, edge_rel, negatives, ovf_src, ovf_dst, ovf_rel, ovf_count):

    def visit(step, carry):
        grad_ent, grad_rel = carry
        bucket = step // N_REL
        group = step % N_REL
        src_base = (bucket * ENT_DEV).astype(jnp.int32)
        dst_base = ((bucket + 1) % N_BUCKET * ENT_DEV).astype(jnp.int32)
        rel_base = (group * REL_DEV).astype(jnp.int32)
        src_tab = lax.dynamic_slice_in_dim(entity, src_base, ENT_DEV, 0)
        dst_tab = lax.dynamic_slice_in_dim(entity, dst_base, ENT_DEV, 0)
        rel_tab = lax.dynamic_slice_in_dim(relation, rel_base, REL_DEV, 0)
        gsrc = jnp.zeros((ENT_DEV, D), jnp.float32)
        gdst = jnp.zeros((ENT_DEV, D), jnp.float32)
        grel = jnp.zeros((REL_DEV, D), jnp.float32)
        for block in range(BLOCKS):
            s_ids = edge_src[bucket, group, block]
            d_ids = edge_dst[bucket, group, block]
            r_ids = edge_rel[bucket, group, block]
            n_ids = negatives[bucket, group, block]
            src_rows = src_tab[s_ids]
            rel_rows = rel_tab[r_ids]
            dq, ddst, dneg = block_grads(src_rows * rel_rows, dst_tab[d_ids], dst_tab[n_ids], 1.0)
            gsrc = gsrc.at[s_ids].add(dq * rel_rows)
            grel = grel.at[r_ids].add(dq * src_rows)
            gdst = gdst.at[d_ids].add(ddst).at[n_ids].add(dneg)
        o_src = ovf_src[bucket, group].reshape(N_SUB * OVF, OCH)
        o_dst = ovf_dst[bucket, group].reshape(N_SUB * OVF, OCH)
        o_rel = ovf_rel[bucket, group].reshape(N_SUB * OVF, OCH)
        counts = ovf_count[group][:, bucket]
        live = (jnp.arange(OVF)[None, :] < counts[:, None]).reshape(N_SUB * OVF).astype(jnp.float32)
        src_rows = src_tab[o_src]
        rel_rows = rel_tab[o_rel]
        dq, ddst = spill_grads(src_rows * rel_rows, dst_tab[o_dst], live)
        gsrc = gsrc.at[o_src.reshape(-1)].add((dq * rel_rows).reshape(-1, D))
        grel = grel.at[o_rel.reshape(-1)].add((dq * src_rows).reshape(-1, D))
        gdst = gdst.at[o_dst.reshape(-1)].add(ddst.reshape(-1, D))
        grad_ent = lax.dynamic_update_slice_in_dim(grad_ent, lax.dynamic_slice_in_dim(grad_ent, src_base, ENT_DEV, 0) + gsrc, src_base, 0)
        grad_ent = lax.dynamic_update_slice_in_dim(grad_ent, lax.dynamic_slice_in_dim(grad_ent, dst_base, ENT_DEV, 0) + gdst, dst_base, 0)
        grad_rel = lax.dynamic_update_slice_in_dim(grad_rel, lax.dynamic_slice_in_dim(grad_rel, rel_base, REL_DEV, 0) + grel, rel_base, 0)
        return (grad_ent, grad_rel)
    start = (jnp.zeros((N_BUCKET * ENT_DEV, D), jnp.float32), jnp.zeros((N_REL * REL_DEV, D), jnp.float32))
    grad_ent, grad_rel = lax.fori_loop(0, N_BUCKET * N_REL, visit, start)
    new_entity, new_entity_acc = adagrad(entity, entity_acc, grad_ent)
    new_relation, new_relation_acc = adagrad(relation, relation_acc, grad_rel)
    return (new_entity, new_entity_acc, new_relation, new_relation_acc)
```

```python
import functools

import jax
import jax.numpy as jnp
from jax import lax
from jax.experimental import pallas as pl
from jax.experimental.pallas import tpu as pltpu
from jax.sharding import PartitionSpec as P

F32 = jnp.float32
BF16 = jnp.bfloat16
LANES = 128
CHUNK = 256


def mm(a, b):
    return jnp.dot(a, b, preferred_element_type=F32)


def mm_nt(a, b):
    return lax.dot_general(a, b, (((1,), (1,)), ((), ())), preferred_element_type=F32)


def split(x):
    hi = x.astype(BF16)
    return hi, (x - hi.astype(F32)).astype(BF16)


def to_column(row, eye):
    return jnp.sum(jnp.where(eye, row, 0.0), axis=1, keepdims=True)


def to_row(column, eye):
    return jnp.sum(jnp.where(eye, column, 0.0), axis=0, keepdims=True)


def remote(src, dst, send, recv, **target):
    return pltpu.make_async_remote_copy(
        src_ref=src,
        dst_ref=dst,
        send_sem=send,
        recv_sem=recv,
        device_id=target,
        device_id_type=pl.DeviceIdType.MESH,
    )


def kernel(
    sizes,
    ent, ent_acc, rel, rel_acc, e_src, e_dst, e_rel, neg, o_src, o_dst, o_rel, count,
    new_ent, new_ent_acc, new_rel, new_rel_acc,
    neg_in, dst_tab, rel_core, rel_in, rel_all, ent_core, ent_in, moved_in, ent_all,
    ids, weight, src_hl, rel_hl, dst_hl, s_rows, r_rows, q_hi, q_lo, d_hot, s_hot, r_hot,
    xr_hi, xr_lo, xs_hi, xs_lo, gt_hi, gt_lo, g_rel, g_ent, share,
    s_neg, r_neg, s_tab, r_tab, s_rc, r_rc, s_rz, r_rz, s_ra, r_ra, s_rf, r_rf,
    s_ec, r_ec, s_ex, r_ex, s_mv, r_mv, s_ea, r_ea, s_ef, r_ef,
):
    n_bucket, n_rel, n_sub = sizes
    me_b = lax.axis_index("bucket")
    me_g = lax.axis_index("rel")
    me_s = lax.axis_index("sub")
    other = 1 - me_s
    ent_rows, width = ent.shape
    rel_rows = rel.shape[0]
    half_e, half_r = ent_rows // n_sub, rel_rows // n_sub
    own_e, own_r = half_e // n_rel, half_r // n_bucket
    spill = o_src.shape[0]
    block = e_src.shape[0] // n_sub
    tiles = block + spill
    edges = tiles * LANES

    def around(me, step, n):
        return lax.rem(me + step, n)

    barrier = pltpu.get_barrier_semaphore()
    for k in range(1, n_bucket):
        pl.semaphore_signal(barrier, inc=1, device_id={"bucket": around(me_b, k, n_bucket)},
                            device_id_type=pl.DeviceIdType.MESH)
    for k in range(1, n_rel):
        pl.semaphore_signal(barrier, inc=1, device_id={"rel": around(me_g, k, n_rel)},
                            device_id_type=pl.DeviceIdType.MESH)
    pl.semaphore_signal(barrier, inc=1, device_id={"sub": other},
                        device_id_type=pl.DeviceIdType.MESH)
    pl.semaphore_wait(barrier, n_bucket - 1 + n_rel - 1 + 1)

    my_half = pl.ds(pl.multiple_of(me_s * half_e, half_e), half_e)
    tab = remote(ent.at[my_half], dst_tab.at[my_half], s_tab.at[0], r_tab.at[0],
                 bucket=around(me_b, n_bucket - 1, n_bucket))
    tab.start()
    negs = remote(neg, neg_in, s_neg, r_neg, sub=other)
    negs.start()

    eye = (lax.broadcasted_iota(jnp.int32, (LANES, LANES), 0)
           == lax.broadcasted_iota(jnp.int32, (LANES, LANES), 1))
    lane_e = lax.broadcasted_iota(jnp.int32, (LANES, ent_rows), 1).astype(F32)
    lane_r = lax.broadcasted_iota(jnp.int32, (LANES, rel_rows), 1).astype(F32)
    sub_e = lax.broadcasted_iota(jnp.int32, (ent_rows, LANES), 0)
    sub_r = lax.broadcasted_iota(jnp.int32, (rel_rows, LANES), 0)

    for place, (mine, over) in enumerate(((e_src, o_src), (e_dst, o_dst), (e_rel, o_rel))):
        for t in range(block):
            ids[place, t] = mine[pl.ds(me_s * block + t, 1), :]
        for t in range(spill):
            ids[place, block + t] = over[pl.ds(t, 1), :]

    src_hl[0], src_hl[1] = split(ent[...])
    rel_hl[0], rel_hl[1] = split(rel[...])
    own = jnp.sum(jnp.where(lax.broadcasted_iota(jnp.int32, count.shape, 1) == me_b, count[...], 0)
                  .astype(F32), axis=1, keepdims=True)

    def gather(t, carry):
        rows = pl.ds(pl.multiple_of(t * LANES, LANES), LANES)
        s_id, d_id, r_id = ids[0, t], ids[1, t], ids[2, t]
        hot = (lane_e == to_column(s_id.astype(F32), eye)).astype(F32).astype(BF16)
        s = mm(hot, src_hl[0]) + mm(hot, src_hl[1])
        hot = (lane_r == to_column(r_id.astype(F32), eye)).astype(F32).astype(BF16)
        r = mm(hot, rel_hl[0]) + mm(hot, rel_hl[1])
        s_rows[rows] = s
        r_rows[rows] = r
        q_hi[rows], q_lo[rows] = split(s * r)
        hot = (lane_e == to_column(d_id.astype(F32), eye)).astype(F32)
        d_hot[rows] = hot
        live = ((t - block).astype(F32) < own).astype(F32)
        weight[t] = jnp.sum(hot, axis=0, keepdims=True) * (live * (1.0 / LANES))
        s_hot[:, rows] = (sub_e == s_id).astype(F32).astype(BF16)
        r_hot[:, rows] = (sub_r == r_id).astype(F32).astype(BF16)
        return carry

    lax.fori_loop(0, tiles, gather, 0)

    negs.wait_recv()
    times = jnp.zeros((1, ent_rows), F32)
    for held in (neg, neg_in):
        for t in range(held.shape[0]):
            column = to_column(held[pl.ds(t, 1), :].astype(F32), eye)
            times += jnp.sum((lane_e == column).astype(F32), axis=0, keepdims=True)
    n_neg = n_sub * neg.shape[0] * LANES
    for t in range(block):
        weight[t] = times * (1.0 / n_neg)

    tab.wait_recv()
    tab_core = remote(dst_tab.at[my_half], dst_tab.at[my_half], s_tab.at[1], r_tab.at[1], sub=other)
    tab_core.start()
    tab_core.wait_recv()
    dst_hl[0], dst_hl[1] = split(dst_tab[...])

    def score(c, carry):
        rows = pl.ds(pl.multiple_of(c * CHUNK, CHUNK), CHUNK)
        q_h, q_l = q_hi[rows], q_lo[rows]
        s = mm_nt(q_h, dst_hl[0]) + mm_nt(q_h, dst_hl[1]) + mm_nt(q_l, dst_hl[0])
        sig = lax.logistic(s)
        per = CHUNK // LANES
        w = jnp.concatenate(
            [jnp.broadcast_to(weight[c * per + i], (LANES, ent_rows)) for i in range(per)], axis=0)
        live = jnp.concatenate(
            [jnp.broadcast_to(((c * per + i - block).astype(F32) < own).astype(F32), (LANES, 1))
             for i in range(per)], axis=0)
        g = sig * w + d_hot[rows] * live * (sig - 1.0)
        g_h, g_l = split(g)
        dq = mm(g_h, dst_hl[0]) + mm(g_h, dst_hl[1]) + mm(g_l, dst_hl[0])
        xr_hi[rows], xr_lo[rows] = split(dq * s_rows[rows])
        xs_hi[rows], xs_lo[rows] = split(dq * r_rows[rows])
        gt_hi[:, rows], gt_lo[:, rows] = split(g.T)
        return carry

    lax.fori_loop(0, edges // CHUNK, score, 0)

    g_rel[...] = mm(r_hot[...], xr_hi[...]) + mm(r_hot[...], xr_lo[...])
    mine_r = pl.ds(pl.multiple_of(me_s * half_r, half_r), half_r)
    twin_r = pl.ds(pl.multiple_of(other * half_r, half_r), half_r)
    rel_c = remote(g_rel.at[twin_r], rel_core, s_rc, r_rc, sub=other)
    rel_c.start()

    g_ent[1] = mm(gt_hi[...], q_hi[...]) + mm(gt_hi[...], q_lo[...]) + mm(gt_lo[...], q_hi[...])
    twin_e = pl.ds(pl.multiple_of(other * half_e, half_e), half_e)

    def to_twin(which):
        copy = remote(g_ent.at[which, twin_e], ent_core.at[which], s_ec.at[which], r_ec.at[which],
                      sub=other)
        copy.start()
        return copy

    def to_rel(which):
        copies = []
        for k in range(1, n_rel):
            peer = around(me_g, k, n_rel)
            there = pl.ds(pl.multiple_of(peer * own_e, own_e), own_e)
            copy = remote(ent_core.at[which, there], ent_in.at[which, k], s_ex.at[which, k],
                          r_ex.at[which, k], rel=peer)
            copy.start()
            copies.append(copy)
        return copies

    here_e = pl.ds(pl.multiple_of(me_g * own_e, own_e), own_e)

    def summed(which, copies):
        total = ent_core[which, here_e]
        for k, copy in enumerate(copies):
            copy.wait_recv()
            total = total + ent_in[which, k + 1]
        return total

    dst_c = to_twin(1)

    rel_c.wait_recv()
    rel_core[...] = rel_core[...] + g_rel[mine_r]
    rel_z = []
    for k in range(1, n_bucket):
        peer = around(me_b, k, n_bucket)
        there = pl.ds(pl.multiple_of(peer * own_r, own_r), own_r)
        copy = remote(rel_core.at[there], rel_in.at[k], s_rz.at[k], r_rz.at[k], bucket=peer)
        copy.start()
        rel_z.append(copy)

    dst_c.wait_recv()
    ent_core[1] = ent_core[1] + g_ent[1, my_half]
    dst_x = to_rel(1)

    g_ent[0] = mm(s_hot[...], xs_hi[...]) + mm(s_hot[...], xs_lo[...])
    src_c = to_twin(0)

    share[...] = summed(1, dst_x)
    moved = remote(share, moved_in, s_mv, r_mv, bucket=around(me_b, 1, n_bucket))
    moved.start()

    src_c.wait_recv()
    ent_core[0] = ent_core[0] + g_ent[0, my_half]
    src_x = to_rel(0)

    total = rel_core[pl.ds(pl.multiple_of(me_b * own_r, own_r), own_r)]
    for k, copy in enumerate(rel_z):
        copy.wait_recv()
        total = total + rel_in[k + 1]

    def rows_r(owner):
        return pl.ds(pl.multiple_of(me_s * half_r + owner * own_r, own_r), own_r)

    rel_all[rows_r(me_b)] = total
    rel_a, rel_f = [], []
    for k in range(1, n_bucket):
        peer = around(me_b, k, n_bucket)
        copy = remote(rel_all.at[rows_r(me_b)], rel_all.at[rows_r(me_b)], s_ra.at[k], r_ra.at[k],
                      bucket=peer)
        copy.start()
        rel_a.append(copy)

    def forward_r(k):
        there = rows_r(around(me_b, n_bucket - k, n_bucket))
        copy = remote(rel_all.at[there], rel_all.at[there], s_rf.at[k], r_rf.at[k], sub=other)
        copy.start()
        rel_f.append(copy)

    forward_r(0)

    def rows_e(owner):
        return pl.ds(pl.multiple_of(me_s * half_e + owner * own_e, own_e), own_e)

    total = summed(0, src_x)
    moved.wait_recv()
    ent_all[rows_e(me_g)] = total + moved_in[...]
    ent_a, ent_f = [], []
    for k in range(1, n_rel):
        peer = around(me_g, k, n_rel)
        copy = remote(ent_all.at[rows_e(me_g)], ent_all.at[rows_e(me_g)], s_ea.at[k], r_ea.at[k],
                      rel=peer)
        copy.start()
        ent_a.append(copy)

    def forward_e(k):
        there = rows_e(around(me_g, n_rel - k, n_rel))
        copy = remote(ent_all.at[there], ent_all.at[there], s_ef.at[k], r_ef.at[k], sub=other)
        copy.start()
        ent_f.append(copy)

    forward_e(0)
    for k in range(1, n_rel):
        ent_a[k - 1].wait_recv()
        forward_e(k)

    def adagrad(table, accum, grads, out, out_acc, t):
        rows = pl.ds(t * LANES, LANES)
        grad = grads[rows]
        fresh = (to_column(accum[pl.ds(t, 1), :], eye)
                 + jnp.sum(grad * grad, axis=1, keepdims=True) * (1.0 / width))
        out[rows] = table[rows] - grad * (0.1 * lax.rsqrt(fresh))
        out_acc[pl.ds(t, 1), :] = to_row(fresh, eye)

    for copy in ent_f:
        copy.wait_recv()
    for t in range(ent_rows // LANES):
        adagrad(ent, ent_acc, ent_all, new_ent, new_ent_acc, t)

    for k in range(1, n_bucket):
        rel_a[k - 1].wait_recv()
        forward_r(k)
    for copy in rel_f:
        copy.wait_recv()
    for t in range(rel_rows // LANES):
        adagrad(rel, rel_acc, rel_all, new_rel, new_rel_acc, t)

    for copy in [tab, negs, tab_core, rel_c, dst_c, src_c, moved] + (
            rel_z + dst_x + src_x + rel_a + rel_f + ent_a + ent_f):
        copy.wait_send()


def body(sizes, entity, entity_acc, relation, relation_acc, edge_src, edge_dst, edge_rel, negatives,
         ovf_src, ovf_dst, ovf_rel, ovf_count):
    n_bucket, n_rel, n_sub = sizes
    ent_rows, width = entity.shape
    rel_rows = relation.shape[0]
    lined = lambda x: x.reshape(-1, LANES)
    half_e, half_r = ent_rows // n_sub, rel_rows // n_sub
    own_e, own_r = half_e // n_rel, half_r // n_bucket
    tiles = edge_src.size // n_sub // LANES + ovf_src.size // LANES
    edges = tiles * LANES
    neg_rows = negatives.size // LANES
    vmem = pltpu.VMEM
    dma = pltpu.SemaphoreType.DMA
    scratch = [
        vmem((neg_rows, LANES), jnp.int32),
        vmem((ent_rows, width), F32),
        vmem((half_r, width), F32),
        vmem((n_bucket, own_r, width), F32),
        vmem((rel_rows, width), F32),
        vmem((2, half_e, width), F32),
        vmem((2, n_rel, own_e, width), F32),
        vmem((own_e, width), F32),
        vmem((ent_rows, width), F32),
        vmem((3, tiles, 1, LANES), jnp.int32),
        vmem((tiles, 1, ent_rows), F32),
        vmem((2, ent_rows, width), BF16),
        vmem((2, rel_rows, width), BF16),
        vmem((2, ent_rows, width), BF16),
        vmem((edges, width), F32),
        vmem((edges, width), F32),
        vmem((edges, width), BF16),
        vmem((edges, width), BF16),
        vmem((edges, ent_rows), F32),
        vmem((ent_rows, edges), BF16),
        vmem((rel_rows, edges), BF16),
        vmem((edges, width), BF16),
        vmem((edges, width), BF16),
        vmem((edges, width), BF16),
        vmem((edges, width), BF16),
        vmem((ent_rows, edges), BF16),
        vmem((ent_rows, edges), BF16),
        vmem((rel_rows, width), F32),
        vmem((2, ent_rows, width), F32),
        vmem((own_e, width), F32),
        dma, dma,
        dma((2,)), dma((2,)),
        dma, dma,
        dma((n_bucket,)), dma((n_bucket,)),
        dma((n_bucket,)), dma((n_bucket,)),
        dma((n_bucket,)), dma((n_bucket,)),
        dma((2,)), dma((2,)),
        dma((2, n_rel)), dma((2, n_rel)),
        dma, dma,
        dma((n_rel,)), dma((n_rel,)),
        dma((n_rel,)), dma((n_rel,)),
    ]
    new_ent, new_ent_acc, new_rel, new_rel_acc = pl.pallas_call(
        functools.partial(kernel, sizes),
        out_shape=(
            jax.ShapeDtypeStruct(entity.shape, F32),
            jax.ShapeDtypeStruct((ent_rows // LANES, LANES), F32),
            jax.ShapeDtypeStruct(relation.shape, F32),
            jax.ShapeDtypeStruct((rel_rows // LANES, LANES), F32),
        ),
        in_specs=[pl.BlockSpec(memory_space=vmem)] * 12,
        out_specs=[pl.BlockSpec(memory_space=vmem)] * 4,
        scratch_shapes=scratch,
        compiler_params=pltpu.CompilerParams(
            collective_id=0, has_side_effects=True, vmem_limit_bytes=40 * 1024 * 1024),
    )(
        entity, lined(entity_acc), relation, lined(relation_acc),
        lined(edge_src), lined(edge_dst), lined(edge_rel), lined(negatives),
        lined(ovf_src), lined(ovf_dst), lined(ovf_rel), ovf_count.reshape(1, -1),
    )
    return new_ent, new_ent_acc.reshape(-1), new_rel, new_rel_acc.reshape(-1)


def solution(mesh):
    sizes = (mesh.shape["bucket"], mesh.shape["rel"], mesh.shape["sub"])
    edge = P(("groups", "bucket"), "rel", None, None)
    over = P(("groups", "bucket"), "rel", "sub", None, None)
    rows = (
        P(("groups", "bucket"), None),
        P(("groups", "bucket")),
        P(("groups", "rel"), None),
        P(("groups", "rel")),
    )
    return jax.shard_map(
        functools.partial(body, sizes),
        mesh=mesh,
        in_specs=rows + (edge, edge, edge, P(("groups", "bucket"), "rel", None, "sub"),
                         over, over, over, P(("groups", "rel"), "sub", None)),
        out_specs=rows,
        check_vma=False,
    )
```

```python
import functools

import jax
import jax.numpy as jnp
from jax import lax
from jax.experimental import pallas as pl
from jax.experimental.pallas import tpu as pltpu
from jax.sharding import PartitionSpec as P

F32 = jnp.float32
BF16 = jnp.bfloat16
LANES = 128
CHUNK = 256


def mm(a, b):
    return jnp.dot(a, b, preferred_element_type=F32)


def mm_nt(a, b):
    return lax.dot_general(a, b, (((1,), (1,)), ((), ())), preferred_element_type=F32)


def split(x):
    hi = x.astype(BF16)
    return hi, (x - hi.astype(F32)).astype(BF16)


def to_column(row, eye):
    return jnp.sum(jnp.where(eye, row, 0.0), axis=1, keepdims=True)


def to_row(column, eye):
    return jnp.sum(jnp.where(eye, column, 0.0), axis=0, keepdims=True)


def remote(src, dst, send, recv, **target):
    return pltpu.make_async_remote_copy(
        src_ref=src,
        dst_ref=dst,
        send_sem=send,
        recv_sem=recv,
        device_id=target,
        device_id_type=pl.DeviceIdType.MESH,
    )


def kernel(
    sizes,
    a_ent, a_ent_acc, a_rel, a_rel_acc, a_src, a_dst, a_typ, a_neg, a_o_src, a_o_dst, a_o_rel, a_count,
    out_ent, out_ent_acc, out_rel, out_rel_acc,
    ent, ent_acc, rel, rel_acc, e_src, e_dst, e_rel, neg, o_src, o_dst, o_rel, count, s_load,
    neg_in, dst_tab, rel_core, rel_in, rel_all, ent_core, ent_in, moved_in, ent_all,
    ids, weight, src_hl, rel_hl, dst_hl, s_rows, r_rows, q_hi, q_lo, d_hot, s_hot, r_hot,
    xr_hi, xr_lo, xs_hi, xs_lo, gt_hi, gt_lo, rel_out, rel_own, g_ent, share,
    ent_new, ent_new_acc, rel_new, rel_new_acc, s_out,
    s_neg, r_neg, s_tab, r_tab, s_rc, r_rc, s_rz, r_rz, s_ra, r_ra, s_rf, r_rf,
    s_ec, r_ec, s_ex, r_ex, s_mv, r_mv, s_ea, r_ea, s_ef, r_ef,
):
    n_bucket, n_rel, n_sub = sizes
    me_b = lax.axis_index("bucket")
    me_g = lax.axis_index("rel")
    me_s = lax.axis_index("sub")
    other = 1 - me_s
    ent_rows, width = ent.shape
    rel_rows = rel.shape[0]
    half_e, half_r = ent_rows // n_sub, rel_rows // n_sub
    own_e, own_r = half_e // n_rel, half_r // n_bucket
    spill = o_src.shape[0]
    block = e_src.shape[0] // n_sub
    tiles = block + spill
    edges = tiles * LANES

    def around(me, step, n):
        return lax.rem(me + step, n)

    loads = [
        pltpu.make_async_copy(there, here, s_load.at[i])
        for i, (there, here) in enumerate((
            (a_src, e_src), (a_dst, e_dst), (a_typ, e_rel), (a_neg, neg), (a_o_src, o_src),
            (a_o_dst, o_dst), (a_o_rel, o_rel), (a_count, count), (a_ent, ent), (a_rel, rel),
            (a_ent_acc, ent_acc), (a_rel_acc, rel_acc)))
    ]
    for copy in loads:
        copy.start()

    barrier = pltpu.get_barrier_semaphore()
    for k in range(1, n_bucket):
        pl.semaphore_signal(barrier, inc=1, device_id={"bucket": around(me_b, k, n_bucket)},
                            device_id_type=pl.DeviceIdType.MESH)
    for k in range(1, n_rel):
        pl.semaphore_signal(barrier, inc=1, device_id={"rel": around(me_g, k, n_rel)},
                            device_id_type=pl.DeviceIdType.MESH)
    pl.semaphore_signal(barrier, inc=1, device_id={"sub": other},
                        device_id_type=pl.DeviceIdType.MESH)
    pl.semaphore_wait(barrier, n_bucket - 1 + n_rel - 1 + 1)

    my_half = pl.ds(pl.multiple_of(me_s * half_e, half_e), half_e)
    tab = remote(a_ent.at[my_half], dst_tab.at[my_half], s_tab.at[0], r_tab.at[0],
                 bucket=around(me_b, n_bucket - 1, n_bucket))
    tab.start()
    negs = remote(a_neg, neg_in, s_neg, r_neg, sub=other)
    negs.start()

    for copy in loads:
        copy.wait()
    eye = (lax.broadcasted_iota(jnp.int32, (LANES, LANES), 0)
           == lax.broadcasted_iota(jnp.int32, (LANES, LANES), 1))
    lane_e = lax.broadcasted_iota(jnp.int32, (LANES, ent_rows), 1).astype(F32)
    lane_r = lax.broadcasted_iota(jnp.int32, (LANES, rel_rows), 1).astype(F32)
    sub_e = lax.broadcasted_iota(jnp.int32, (ent_rows, LANES), 0)
    sub_r = lax.broadcasted_iota(jnp.int32, (rel_rows, LANES), 0)

    for place, (mine, over) in enumerate(((e_src, o_src), (e_dst, o_dst), (e_rel, o_rel))):
        for t in range(block):
            ids[place, t] = mine[pl.ds(me_s * block + t, 1), :]
        for t in range(spill):
            ids[place, block + t] = over[pl.ds(t, 1), :]

    src_hl[0], src_hl[1] = split(ent[...])
    rel_hl[0], rel_hl[1] = split(rel[...])
    own = jnp.sum(jnp.where(lax.broadcasted_iota(jnp.int32, count.shape, 1) == me_b, count[...], 0)
                  .astype(F32), axis=1, keepdims=True)

    def gather(t, carry):
        rows = pl.ds(pl.multiple_of(t * LANES, LANES), LANES)
        s_id, d_id, r_id = ids[0, t], ids[1, t], ids[2, t]
        hot = (lane_e == to_column(s_id.astype(F32), eye)).astype(F32).astype(BF16)
        s = mm(hot, src_hl[0]) + mm(hot, src_hl[1])
        hot = (lane_r == to_column(r_id.astype(F32), eye)).astype(F32).astype(BF16)
        r = mm(hot, rel_hl[0]) + mm(hot, rel_hl[1])
        s_rows[rows] = s
        r_rows[rows] = r
        q_hi[rows], q_lo[rows] = split(s * r)
        hot = (lane_e == to_column(d_id.astype(F32), eye)).astype(F32)
        d_hot[rows] = hot
        live = ((t - block).astype(F32) < own).astype(F32)
        weight[t] = jnp.sum(hot, axis=0, keepdims=True) * (live * (1.0 / LANES))
        s_hot[:, rows] = (sub_e == s_id).astype(F32).astype(BF16)
        r_hot[:, rows] = (sub_r == r_id).astype(F32).astype(BF16)
        return carry

    lax.fori_loop(0, tiles, gather, 0)

    negs.wait_recv()
    times = jnp.zeros((1, ent_rows), F32)
    for held in (neg, neg_in):
        for t in range(held.shape[0]):
            column = to_column(held[pl.ds(t, 1), :].astype(F32), eye)
            times += jnp.sum((lane_e == column).astype(F32), axis=0, keepdims=True)
    n_neg = n_sub * neg.shape[0] * LANES
    for t in range(block):
        weight[t] = times * (1.0 / n_neg)

    tab.wait_recv()
    tab_core = remote(dst_tab.at[my_half], dst_tab.at[my_half], s_tab.at[1], r_tab.at[1], sub=other)
    tab_core.start()
    tab_core.wait_recv()
    dst_hl[0], dst_hl[1] = split(dst_tab[...])

    def score(c, carry):
        rows = pl.ds(pl.multiple_of(c * CHUNK, CHUNK), CHUNK)
        q_h, q_l = q_hi[rows], q_lo[rows]
        s = mm_nt(q_h, dst_hl[0]) + mm_nt(q_h, dst_hl[1]) + mm_nt(q_l, dst_hl[0])
        sig = lax.logistic(s)
        per = CHUNK // LANES
        w = jnp.concatenate(
            [jnp.broadcast_to(weight[c * per + i], (LANES, ent_rows)) for i in range(per)], axis=0)
        live = jnp.concatenate(
            [jnp.broadcast_to(((c * per + i - block).astype(F32) < own).astype(F32), (LANES, 1))
             for i in range(per)], axis=0)
        g = sig * w + d_hot[rows] * live * (sig - 1.0)
        g_h, g_l = split(g)
        dq = mm(g_h, dst_hl[0]) + mm(g_h, dst_hl[1]) + mm(g_l, dst_hl[0])
        xr_hi[rows], xr_lo[rows] = split(dq * s_rows[rows])
        xs_hi[rows], xs_lo[rows] = split(dq * r_rows[rows])
        gt_hi[:, rows], gt_lo[:, rows] = split(g.T)
        return carry

    lax.fori_loop(0, edges // CHUNK, score, 0, unroll=True)

    mine_r, twin_r = me_s * half_r, other * half_r
    hop, cut = n_bucket // 2, own_r // 2

    def part(base, k, half=None):
        first = base + around(me_b, k % n_bucket, n_bucket) * own_r
        if half is None:
            return pl.ds(pl.multiple_of(first, own_r), own_r)
        return pl.ds(pl.multiple_of(first + half * cut, cut), cut)

    def scatter_r(base):
        hot = r_hot[pl.ds(pl.multiple_of(base, half_r), half_r), :]
        return mm(hot, xr_hi[...]) + mm(hot, xr_lo[...])

    rel_out[...] = scatter_r(twin_r)
    order = [hop] + [k * way for k in range(hop - 1, 0, -1) for way in (1, -1)] + [0]
    rel_c = {}
    for i, k in enumerate(order):
        copy = remote(rel_out.at[part(0, k)], rel_core.at[part(0, k)], s_rc.at[i], r_rc.at[i],
                      sub=other)
        copy.start()
        rel_c[k] = copy
    rel_own[...] = scatter_r(mine_r)

    def of_chip(k):
        rel_c[k].wait_recv()
        rel_core[part(0, k)] = rel_core[part(0, k)] + rel_own[part(0, k)]

    def toward(way):
        return around(me_b, 1 if way == 0 else n_bucket - 1, n_bucket)

    rel_z = {}

    def pass_on(way, half, t):
        k = (hop - t) * (1 if way == 0 else -1)
        rows = part(0, k, half)
        if (way, half, t - 1) in rel_z:
            rel_z[way, half, t - 1].wait_recv()
            rel_core[rows] = rel_core[rows] + rel_in[way, half, t - 1]
        copy = remote(rel_core.at[rows], rel_in.at[way, half, t], s_rz.at[way, half, t],
                      r_rz.at[way, half, t], bucket=toward(way))
        copy.start()
        rel_z[way, half, t] = copy

    of_chip(hop)
    for way in range(2):
        pass_on(way, way, 0)
    if hop > 1:
        for way, k in ((0, hop - 1), (1, 1 - hop)):
            of_chip(k)
            pass_on(way, 1 - way, 1)

    g_ent[1] = mm(gt_hi[...], q_hi[...]) + mm(gt_hi[...], q_lo[...]) + mm(gt_lo[...], q_hi[...])
    twin_e = pl.ds(pl.multiple_of(other * half_e, half_e), half_e)

    def to_twin(which):
        copy = remote(g_ent.at[which, twin_e], ent_core.at[which], s_ec.at[which], r_ec.at[which],
                      sub=other)
        copy.start()
        return copy

    def to_rel(which):
        copies = []
        for k in range(1, n_rel):
            peer = around(me_g, k, n_rel)
            there = pl.ds(pl.multiple_of(peer * own_e, own_e), own_e)
            copy = remote(ent_core.at[which, there], ent_in.at[which, k], s_ex.at[which, k],
                          r_ex.at[which, k], rel=peer)
            copy.start()
            copies.append(copy)
        return copies

    here_e = pl.ds(pl.multiple_of(me_g * own_e, own_e), own_e)

    def summed(which, copies):
        total = ent_core[which, here_e]
        for k, copy in enumerate(copies):
            copy.wait_recv()
            total = total + ent_in[which, k + 1]
        return total

    dst_c = to_twin(1)

    if hop > 1:
        for way in range(2):
            pass_on(way, way, 1)

    g_ent[0] = mm(s_hot[...], xs_hi[...]) + mm(s_hot[...], xs_lo[...])
    src_c = to_twin(0)

    dst_c.wait_recv()
    ent_core[1] = ent_core[1] + g_ent[1, my_half]
    dst_x = to_rel(1)

    for t in range(2, hop):
        for way, k in ((0, hop - t), (1, t - hop)):
            of_chip(k)
            for half in (way, 1 - way):
                pass_on(way, half, t)
    of_chip(0)

    for half in range(2):
        total = rel_core[part(0, 0, half)]
        for way in range(2):
            if (way, half, hop - 1) in rel_z:
                rel_z[way, half, hop - 1].wait_recv()
                total = total + rel_in[way, half, hop - 1]
        rel_all[part(mine_r, 0, half)] = total
    rel_a, rel_f = {}, []

    def hand_on(way, t):
        rows = part(mine_r, -t if way == 0 else t, way if t == hop - 1 else None)
        copy = remote(rel_all.at[rows], rel_all.at[rows], s_ra.at[way, t], r_ra.at[way, t],
                      bucket=toward(way))
        copy.start()
        rel_a[way, t] = copy

    def forward_r(rows):
        i = len(rel_f)
        copy = remote(rel_all.at[rows], rel_all.at[rows], s_rf.at[i], r_rf.at[i], sub=other)
        copy.start()
        rel_f.append(copy)

    for way in range(2):
        hand_on(way, 0)
    forward_r(part(mine_r, 0))

    src_c.wait_recv()
    ent_core[0] = ent_core[0] + g_ent[0, my_half]
    src_x = to_rel(0)

    share[...] = summed(1, dst_x)
    moved = remote(share, moved_in, s_mv, r_mv, bucket=around(me_b, 1, n_bucket))
    moved.start()

    for t in range(1, hop):
        for way in range(2):
            rel_a[way, t - 1].wait_recv()
            hand_on(way, t)
            forward_r(part(mine_r, -t if way == 0 else t))

    def rows_e(owner):
        return pl.ds(pl.multiple_of(me_s * half_e + owner * own_e, own_e), own_e)

    total = summed(0, src_x)
    moved.wait_recv()
    ent_all[rows_e(me_g)] = total + moved_in[...]
    ent_a, ent_f = [], []
    for k in range(1, n_rel):
        peer = around(me_g, k, n_rel)
        copy = remote(ent_all.at[rows_e(me_g)], ent_all.at[rows_e(me_g)], s_ea.at[k], r_ea.at[k],
                      rel=peer)
        copy.start()
        ent_a.append(copy)

    def forward_e(k):
        there = rows_e(around(me_g, n_rel - k, n_rel))
        copy = remote(ent_all.at[there], ent_all.at[there], s_ef.at[k], r_ef.at[k], sub=other)
        copy.start()
        ent_f.append(copy)

    forward_e(0)

    for way in range(2):
        rel_a[way, hop - 1].wait_recv()
        forward_r(part(mine_r, -hop if way == 0 else hop, way))

    stores = []

    def adagrad(table, accum, grads, staged, staged_acc, out, first, count, sem):
        first = pl.multiple_of(first, count)
        for i in range(count // LANES):
            rows = pl.ds(pl.multiple_of(first + i * LANES, LANES), LANES)
            at = pl.ds(first // LANES + i, 1)
            grad = grads[rows]
            fresh = (to_column(accum[at, :], eye)
                     + jnp.sum(grad * grad, axis=1, keepdims=True) * (1.0 / width))
            staged[rows] = table[rows] - grad * (0.1 * lax.rsqrt(fresh))
            staged_acc[at, :] = to_row(fresh, eye)
        whole = pl.ds(first, count)
        copy = pltpu.make_async_copy(staged.at[whole], out.at[whole], s_out.at[sem])
        copy.start()
        stores.append(copy)

    adagrad(rel, rel_acc, rel_all, rel_new, rel_new_acc, out_rel, mine_r, half_r, 0)
    for k in range(1, n_rel):
        ent_a[k - 1].wait_recv()
        forward_e(k)
    adagrad(ent, ent_acc, ent_all, ent_new, ent_new_acc, out_ent, me_s * half_e, half_e, 1)
    for copy in rel_f:
        copy.wait_recv()
    adagrad(rel, rel_acc, rel_all, rel_new, rel_new_acc, out_rel, twin_r, half_r, 2)
    for copy in ent_f:
        copy.wait_recv()
    adagrad(ent, ent_acc, ent_all, ent_new, ent_new_acc, out_ent, other * half_e, half_e, 3)
    for i, (here, there) in enumerate(((rel_new_acc, out_rel_acc), (ent_new_acc, out_ent_acc))):
        copy = pltpu.make_async_copy(here, there, s_out.at[4 + i])
        copy.start()
        stores.append(copy)

    for copy in [tab, negs, tab_core, dst_c, src_c, moved] + (
            list(rel_c.values()) + list(rel_z.values()) + list(rel_a.values())
            + dst_x + src_x + rel_f + ent_a + ent_f):
        copy.wait_send()
    for copy in stores:
        copy.wait()


def store(*refs):
    sems = refs[-1]
    copies = [pltpu.make_async_copy(refs[i], refs[4 + i], sems.at[i]) for i in range(4)]
    for copy in copies:
        copy.start()
    for copy in copies:
        copy.wait()


def body(sizes, entity, entity_acc, relation, relation_acc, edge_src, edge_dst, edge_rel, negatives,
         ovf_src, ovf_dst, ovf_rel, ovf_count):
    n_bucket, n_rel, n_sub = sizes
    ent_rows, width = entity.shape
    rel_rows = relation.shape[0]
    lined = lambda x: x.reshape(-1, LANES)
    half_e, half_r = ent_rows // n_sub, rel_rows // n_sub
    own_e, own_r = half_e // n_rel, half_r // n_bucket
    tiles = edge_src.size // n_sub // LANES + ovf_src.size // LANES
    edges = tiles * LANES
    neg_rows = negatives.size // LANES
    hop = n_bucket // 2
    vmem = pltpu.VMEM
    dma = pltpu.SemaphoreType.DMA
    args = (
        entity, lined(entity_acc), relation, lined(relation_acc),
        lined(edge_src), lined(edge_dst), lined(edge_rel), lined(negatives),
        lined(ovf_src), lined(ovf_dst), lined(ovf_rel), ovf_count.reshape(1, -1),
    )
    scratch = [vmem(arg.shape, arg.dtype) for arg in args] + [dma((len(args),))] + [
        vmem((neg_rows, LANES), jnp.int32),
        vmem((ent_rows, width), F32),
        vmem((half_r, width), F32),
        vmem((2, 2, hop, own_r // 2, width), F32),
        vmem((rel_rows, width), F32),
        vmem((2, half_e, width), F32),
        vmem((2, n_rel, own_e, width), F32),
        vmem((own_e, width), F32),
        vmem((ent_rows, width), F32),
        vmem((3, tiles, 1, LANES), jnp.int32),
        vmem((tiles, 1, ent_rows), F32),
        vmem((2, ent_rows, width), BF16),
        vmem((2, rel_rows, width), BF16),
        vmem((2, ent_rows, width), BF16),
        vmem((edges, width), F32),
        vmem((edges, width), F32),
        vmem((edges, width), BF16),
        vmem((edges, width), BF16),
        vmem((edges, ent_rows), F32),
        vmem((ent_rows, edges), BF16),
        vmem((rel_rows, edges), BF16),
        vmem((edges, width), BF16),
        vmem((edges, width), BF16),
        vmem((edges, width), BF16),
        vmem((edges, width), BF16),
        vmem((ent_rows, edges), BF16),
        vmem((ent_rows, edges), BF16),
        vmem((half_r, width), F32),
        vmem((half_r, width), F32),
        vmem((2, ent_rows, width), F32),
        vmem((own_e, width), F32),
        vmem(args[0].shape, F32), vmem(args[1].shape, F32),
        vmem(args[2].shape, F32), vmem(args[3].shape, F32),
        dma((6,)),
        dma, dma,
        dma((2,)), dma((2,)),
        dma((n_bucket,)), dma((n_bucket,)),
        dma((2, 2, hop)), dma((2, 2, hop)),
        dma((2, hop)), dma((2, hop)),
        dma((n_bucket + 1,)), dma((n_bucket + 1,)),
        dma((2,)), dma((2,)),
        dma((2, n_rel)), dma((2, n_rel)),
        dma, dma,
        dma((n_rel,)), dma((n_rel,)),
        dma((n_rel,)), dma((n_rel,)),
    ]
    out_shape = tuple(jax.ShapeDtypeStruct(arg.shape, F32) for arg in args[:4])
    made = pl.pallas_call(
        functools.partial(kernel, sizes),
        out_shape=out_shape,
        in_specs=[pl.BlockSpec(memory_space=pltpu.HBM)] * len(args),
        out_specs=[pl.BlockSpec(memory_space=pltpu.HBM)] * 4,
        scratch_shapes=scratch,
        compiler_params=pltpu.CompilerParams(
            collective_id=0, has_side_effects=True, vmem_limit_bytes=60 * 1024 * 1024),
    )(*args)
    new_ent, new_ent_acc, new_rel, new_rel_acc = pl.pallas_call(
        store,
        out_shape=out_shape,
        in_specs=[pl.BlockSpec(memory_space=pltpu.HBM)] * 4,
        out_specs=[pl.BlockSpec(memory_space=pltpu.HBM)] * 4,
        scratch_shapes=[dma((4,))],
        compiler_params=pltpu.CompilerParams(vmem_limit_bytes=60 * 1024 * 1024),
    )(*made)
    return new_ent, new_ent_acc.reshape(-1), new_rel, new_rel_acc.reshape(-1)


def solution(mesh):
    sizes = (mesh.shape["bucket"], mesh.shape["rel"], mesh.shape["sub"])
    edge = P(("groups", "bucket"), "rel", None, None)
    over = P(("groups", "bucket"), "rel", "sub", None, None)
    rows = (
        P(("groups", "bucket"), None),
        P(("groups", "bucket")),
        P(("groups", "rel"), None),
        P(("groups", "rel")),
    )
    return jax.shard_map(
        functools.partial(body, sizes),
        mesh=mesh,
        in_specs=rows + (edge, edge, edge, P(("groups", "bucket"), "rel", None, "sub"),
                         over, over, over, P(("groups", "rel"), "sub", None)),
        out_specs=rows,
        check_vma=False,
    )
```

```python
import functools

import jax
import jax.numpy as jnp
from jax import lax
from jax.experimental import pallas as pl
from jax.experimental.pallas import tpu as pltpu
from jax.sharding import PartitionSpec as P

F32 = jnp.float32
BF16 = jnp.bfloat16
LANES = 128
CHUNK = 256


def mm(a, b):
    return jnp.dot(a, b, preferred_element_type=F32)


def mm_nt(a, b):
    return lax.dot_general(a, b, (((1,), (1,)), ((), ())), preferred_element_type=F32)


def split(x):
    hi = x.astype(BF16)
    return hi, (x - hi.astype(F32)).astype(BF16)


def to_column(row, eye):
    return jnp.sum(jnp.where(eye, row, 0.0), axis=1, keepdims=True)


def to_row(column, eye):
    return jnp.sum(jnp.where(eye, column, 0.0), axis=0, keepdims=True)


def remote(src, dst, send, recv, **target):
    return pltpu.make_async_remote_copy(
        src_ref=src,
        dst_ref=dst,
        send_sem=send,
        recv_sem=recv,
        device_id=target,
        device_id_type=pl.DeviceIdType.MESH,
    )


def kernel(
    sizes,
    a_ent, a_ent_acc, a_rel, a_rel_acc, a_src, a_dst, a_typ, a_neg, a_o_src, a_o_dst, a_o_rel, a_count,
    out_ent, out_ent_acc, out_rel, out_rel_acc,
    ent, ent_acc, rel, rel_acc, e_src, e_dst, e_rel, neg, o_src, o_dst, o_rel, count, s_load,
    neg_in, dst_tab, rel_core, rel_in, rel_all, ent_core, ent_in, moved_in, ent_all,
    ids, weight, src_hl, rel_hl, dst_hl, s_rows, r_rows, q_hi, q_lo, d_hot, s_hot, r_hot,
    xr_hi, xr_lo, xs_hi, xs_lo, gt_hi, gt_lo, rel_out, rel_own, g_ent, share,
    ent_new, ent_new_acc, rel_new, rel_new_acc, s_out,
    s_neg, r_neg, s_tab, r_tab, s_rc, r_rc, s_rz, r_rz, s_ra, r_ra, s_rf, r_rf,
    s_ec, r_ec, s_ex, r_ex, s_mv, r_mv, s_ea, r_ea, s_ef, r_ef,
):
    n_bucket, n_rel, n_sub = sizes
    me_b = lax.axis_index("bucket")
    me_g = lax.axis_index("rel")
    me_s = lax.axis_index("sub")
    other = 1 - me_s
    ent_rows, width = ent.shape
    rel_rows = rel.shape[0]
    half_e, half_r = ent_rows // n_sub, rel_rows // n_sub
    own_e, own_r = half_e // n_rel, half_r // n_bucket
    spill = o_src.shape[0]
    block = e_src.shape[0] // n_sub
    tiles = block + spill
    edges = tiles * LANES

    def around(me, step, n):
        return lax.rem(me + step, n)

    loads = [
        pltpu.make_async_copy(there, here, s_load.at[i])
        for i, (there, here) in enumerate((
            (a_src, e_src), (a_dst, e_dst), (a_typ, e_rel), (a_neg, neg), (a_o_src, o_src),
            (a_o_dst, o_dst), (a_o_rel, o_rel), (a_count, count), (a_ent, ent), (a_rel, rel),
            (a_ent_acc, ent_acc), (a_rel_acc, rel_acc)))
    ]
    for copy in loads:
        copy.start()

    barrier = pltpu.get_barrier_semaphore()
    for k in range(1, n_bucket):
        pl.semaphore_signal(barrier, inc=1, device_id={"bucket": around(me_b, k, n_bucket)},
                            device_id_type=pl.DeviceIdType.MESH)
    for k in range(1, n_rel):
        pl.semaphore_signal(barrier, inc=1, device_id={"rel": around(me_g, k, n_rel)},
                            device_id_type=pl.DeviceIdType.MESH)
    pl.semaphore_signal(barrier, inc=1, device_id={"sub": other},
                        device_id_type=pl.DeviceIdType.MESH)
    pl.semaphore_wait(barrier, n_bucket - 1 + n_rel - 1 + 1)

    my_half = pl.ds(pl.multiple_of(me_s * half_e, half_e), half_e)
    tab = remote(a_ent.at[my_half], dst_tab.at[my_half], s_tab.at[0], r_tab.at[0],
                 bucket=around(me_b, n_bucket - 1, n_bucket))
    tab.start()
    negs = remote(a_neg, neg_in, s_neg, r_neg, sub=other)
    negs.start()

    for copy in loads:
        copy.wait()
    eye = (lax.broadcasted_iota(jnp.int32, (LANES, LANES), 0)
           == lax.broadcasted_iota(jnp.int32, (LANES, LANES), 1))
    lane_e = lax.broadcasted_iota(jnp.int32, (LANES, ent_rows), 1).astype(F32)
    lane_r = lax.broadcasted_iota(jnp.int32, (LANES, rel_rows), 1).astype(F32)
    sub_e = lax.broadcasted_iota(jnp.int32, (ent_rows, LANES), 0)
    sub_r = lax.broadcasted_iota(jnp.int32, (rel_rows, LANES), 0)

    for place, (mine, over) in enumerate(((e_src, o_src), (e_dst, o_dst), (e_rel, o_rel))):
        for t in range(block):
            ids[place, t] = mine[pl.ds(me_s * block + t, 1), :]
        for t in range(spill):
            ids[place, block + t] = over[pl.ds(t, 1), :]

    src_hl[0], src_hl[1] = split(ent[...])
    rel_hl[0], rel_hl[1] = split(rel[...])
    own = jnp.sum(jnp.where(lax.broadcasted_iota(jnp.int32, count.shape, 1) == me_b, count[...], 0)
                  .astype(F32), axis=1, keepdims=True)

    def gather(t, carry):
        rows = pl.ds(pl.multiple_of(t * LANES, LANES), LANES)
        s_id, d_id, r_id = ids[0, t], ids[1, t], ids[2, t]
        hot = (lane_e == to_column(s_id.astype(F32), eye)).astype(F32).astype(BF16)
        s = mm(hot, src_hl[0]) + mm(hot, src_hl[1])
        hot = (lane_r == to_column(r_id.astype(F32), eye)).astype(F32).astype(BF16)
        r = mm(hot, rel_hl[0]) + mm(hot, rel_hl[1])
        s_rows[rows] = s
        r_rows[rows] = r
        q_hi[rows], q_lo[rows] = split(s * r)
        hot = (lane_e == to_column(d_id.astype(F32), eye)).astype(F32)
        d_hot[rows] = hot
        live = ((t - block).astype(F32) < own).astype(F32)
        weight[t] = jnp.sum(hot, axis=0, keepdims=True) * (live * (1.0 / LANES))
        s_hot[:, rows] = (sub_e == s_id).astype(F32).astype(BF16)
        r_hot[:, rows] = (sub_r == r_id).astype(F32).astype(BF16)
        return carry

    lax.fori_loop(0, tiles, gather, 0)

    negs.wait_recv()
    times = jnp.zeros((1, ent_rows), F32)
    for held in (neg, neg_in):
        for t in range(held.shape[0]):
            column = to_column(held[pl.ds(t, 1), :].astype(F32), eye)
            times += jnp.sum((lane_e == column).astype(F32), axis=0, keepdims=True)
    n_neg = n_sub * neg.shape[0] * LANES
    for t in range(block):
        weight[t] = times * (1.0 / n_neg)

    tab.wait_recv()
    tab_core = remote(dst_tab.at[my_half], dst_tab.at[my_half], s_tab.at[1], r_tab.at[1], sub=other)
    tab_core.start()
    tab_core.wait_recv()
    dst_hl[0], dst_hl[1] = split(dst_tab[...])

    def score(c, carry):
        rows = pl.ds(pl.multiple_of(c * CHUNK, CHUNK), CHUNK)
        q_h, q_l = q_hi[rows], q_lo[rows]
        s = mm_nt(q_h, dst_hl[0]) + mm_nt(q_h, dst_hl[1]) + mm_nt(q_l, dst_hl[0])
        sig = lax.logistic(s)
        per = CHUNK // LANES
        w = jnp.concatenate(
            [jnp.broadcast_to(weight[c * per + i], (LANES, ent_rows)) for i in range(per)], axis=0)
        live = jnp.concatenate(
            [jnp.broadcast_to(((c * per + i - block).astype(F32) < own).astype(F32), (LANES, 1))
             for i in range(per)], axis=0)
        g = sig * w + d_hot[rows] * live * (sig - 1.0)
        g_h, g_l = split(g)
        dq = mm(g_h, dst_hl[0]) + mm(g_h, dst_hl[1]) + mm(g_l, dst_hl[0])
        xr_hi[rows], xr_lo[rows] = split(dq * s_rows[rows])
        xs_hi[rows], xs_lo[rows] = split(dq * r_rows[rows])
        gt_hi[:, rows], gt_lo[:, rows] = split(g.T)
        return carry

    lax.fori_loop(0, edges // CHUNK, score, 0, unroll=True)

    mine_r, twin_r = me_s * half_r, other * half_r

    def part(base, k):
        first = base + around(me_b, k % n_bucket, n_bucket) * own_r
        return pl.ds(pl.multiple_of(first, own_r), own_r)

    def scatter_r(base):
        hot = r_hot[pl.ds(pl.multiple_of(base, half_r), half_r), :]
        return mm(hot, xr_hi[...]) + mm(hot, xr_lo[...])

    rel_out[...] = scatter_r(twin_r)
    order = sorted(range(1, n_bucket), key=lambda k: -min(k, n_bucket - k)) + [0]
    rel_c = {}
    for i, k in enumerate(order):
        copy = remote(rel_out.at[part(0, k)], rel_core.at[part(0, k)], s_rc.at[i], r_rc.at[i],
                      sub=other)
        copy.start()
        rel_c[k] = copy

    g_ent[1] = mm(gt_hi[...], q_hi[...]) + mm(gt_hi[...], q_lo[...]) + mm(gt_lo[...], q_hi[...])
    twin_e = pl.ds(pl.multiple_of(other * half_e, half_e), half_e)

    def to_twin(which):
        copy = remote(g_ent.at[which, twin_e], ent_core.at[which], s_ec.at[which], r_ec.at[which],
                      sub=other)
        copy.start()
        return copy

    def to_rel(which):
        copies = []
        for k in range(1, n_rel):
            peer = around(me_g, k, n_rel)
            there = pl.ds(pl.multiple_of(peer * own_e, own_e), own_e)
            copy = remote(ent_core.at[which, there], ent_in.at[which, k], s_ex.at[which, k],
                          r_ex.at[which, k], rel=peer)
            copy.start()
            copies.append(copy)
        return copies

    here_e = pl.ds(pl.multiple_of(me_g * own_e, own_e), own_e)

    def summed(which, copies):
        total = ent_core[which, here_e]
        for k, copy in enumerate(copies):
            copy.wait_recv()
            total = total + ent_in[which, k + 1]
        return total

    dst_c = to_twin(1)

    rel_own[...] = scatter_r(mine_r)

    def of_chip(k):
        rel_c[k].wait_recv()
        rel_core[part(0, k)] = rel_core[part(0, k)] + rel_own[part(0, k)]

    rel_z = []
    for k in order[:-1]:
        of_chip(k)
        slot = k % n_bucket
        copy = remote(rel_core.at[part(0, k)], rel_in.at[slot], s_rz.at[slot], r_rz.at[slot],
                      bucket=around(me_b, slot, n_bucket))
        copy.start()
        rel_z.append((slot, copy))
    of_chip(0)

    dst_c.wait_recv()
    ent_core[1] = ent_core[1] + g_ent[1, my_half]
    dst_x = to_rel(1)
    g_ent[0] = mm(s_hot[...], xs_hi[...]) + mm(s_hot[...], xs_lo[...])
    src_c = to_twin(0)

    src_c.wait_recv()
    ent_core[0] = ent_core[0] + g_ent[0, my_half]
    src_x = to_rel(0)

    share[...] = summed(1, dst_x)
    moved = remote(share, moved_in, s_mv, r_mv, bucket=around(me_b, 1, n_bucket))
    moved.start()

    total = rel_core[part(0, 0)]
    for slot, copy in rel_z:
        copy.wait_recv()
        total = total + rel_in[slot]
    rel_all[part(mine_r, 0)] = total
    rel_a, rel_f = [], []
    for k in order[:-1]:
        slot = k % n_bucket
        copy = remote(rel_all.at[part(mine_r, 0)], rel_all.at[part(mine_r, 0)], s_ra.at[slot],
                      r_ra.at[slot], bucket=around(me_b, slot, n_bucket))
        copy.start()
        rel_a.append((slot, copy))

    def forward_r(rows):
        i = len(rel_f)
        copy = remote(rel_all.at[rows], rel_all.at[rows], s_rf.at[i], r_rf.at[i], sub=other)
        copy.start()
        rel_f.append(copy)

    forward_r(part(mine_r, 0))

    def rows_e(owner):
        return pl.ds(pl.multiple_of(me_s * half_e + owner * own_e, own_e), own_e)

    total = summed(0, src_x)
    moved.wait_recv()
    ent_all[rows_e(me_g)] = total + moved_in[...]
    ent_a, ent_f = [], []
    for k in range(1, n_rel):
        peer = around(me_g, k, n_rel)
        copy = remote(ent_all.at[rows_e(me_g)], ent_all.at[rows_e(me_g)], s_ea.at[k], r_ea.at[k],
                      rel=peer)
        copy.start()
        ent_a.append(copy)

    def forward_e(k):
        there = rows_e(around(me_g, n_rel - k, n_rel))
        copy = remote(ent_all.at[there], ent_all.at[there], s_ef.at[k], r_ef.at[k], sub=other)
        copy.start()
        ent_f.append(copy)

    forward_e(0)

    for slot, copy in reversed(rel_a):
        copy.wait_recv()
        forward_r(part(mine_r, -slot))

    stores = []

    def adagrad(table, accum, grads, staged, staged_acc, out, first, count, sem):
        first = pl.multiple_of(first, count)
        for i in range(count // LANES):
            rows = pl.ds(pl.multiple_of(first + i * LANES, LANES), LANES)
            at = pl.ds(first // LANES + i, 1)
            grad = grads[rows]
            fresh = (to_column(accum[at, :], eye)
                     + jnp.sum(grad * grad, axis=1, keepdims=True) * (1.0 / width))
            staged[rows] = table[rows] - grad * (0.1 * lax.rsqrt(fresh))
            staged_acc[at, :] = to_row(fresh, eye)
        whole = pl.ds(first, count)
        copy = pltpu.make_async_copy(staged.at[whole], out.at[whole], s_out.at[sem])
        copy.start()
        stores.append(copy)

    adagrad(rel, rel_acc, rel_all, rel_new, rel_new_acc, out_rel, mine_r, half_r, 0)
    for k in range(1, n_rel):
        ent_a[k - 1].wait_recv()
        forward_e(k)
    adagrad(ent, ent_acc, ent_all, ent_new, ent_new_acc, out_ent, me_s * half_e, half_e, 1)
    for copy in rel_f:
        copy.wait_recv()
    adagrad(rel, rel_acc, rel_all, rel_new, rel_new_acc, out_rel, twin_r, half_r, 2)
    for copy in ent_f:
        copy.wait_recv()
    adagrad(ent, ent_acc, ent_all, ent_new, ent_new_acc, out_ent, other * half_e, half_e, 3)
    for i, (here, there) in enumerate(((rel_new_acc, out_rel_acc), (ent_new_acc, out_ent_acc))):
        copy = pltpu.make_async_copy(here, there, s_out.at[4 + i])
        copy.start()
        stores.append(copy)

    for copy in [tab, negs, tab_core, dst_c, src_c, moved] + (
            list(rel_c.values()) + [copy for _, copy in rel_z + rel_a]
            + dst_x + src_x + rel_f + ent_a + ent_f):
        copy.wait_send()
    for copy in stores:
        copy.wait()


def store(*refs):
    made, out, held, sems = refs[:4], refs[4:8], refs[8:12], refs[12]
    loads = [pltpu.make_async_copy(made[i], held[i], sems.at[0, i]) for i in range(4)]
    stores = [pltpu.make_async_copy(held[i], out[i], sems.at[1, i]) for i in range(4)]
    for load in loads:
        load.start()
    for load, copy in zip(loads, stores):
        load.wait()
        copy.start()
    for copy in stores:
        copy.wait()


def body(sizes, entity, entity_acc, relation, relation_acc, edge_src, edge_dst, edge_rel, negatives,
         ovf_src, ovf_dst, ovf_rel, ovf_count):
    n_bucket, n_rel, n_sub = sizes
    ent_rows, width = entity.shape
    rel_rows = relation.shape[0]
    lined = lambda x: x.reshape(-1, LANES)
    half_e, half_r = ent_rows // n_sub, rel_rows // n_sub
    own_e, own_r = half_e // n_rel, half_r // n_bucket
    tiles = edge_src.size // n_sub // LANES + ovf_src.size // LANES
    edges = tiles * LANES
    neg_rows = negatives.size // LANES
    vmem = pltpu.VMEM
    dma = pltpu.SemaphoreType.DMA
    args = (
        entity, lined(entity_acc), relation, lined(relation_acc),
        lined(edge_src), lined(edge_dst), lined(edge_rel), lined(negatives),
        lined(ovf_src), lined(ovf_dst), lined(ovf_rel), ovf_count.reshape(1, -1),
    )
    scratch = [vmem(arg.shape, arg.dtype) for arg in args] + [dma((len(args),))] + [
        vmem((neg_rows, LANES), jnp.int32),
        vmem((ent_rows, width), F32),
        vmem((half_r, width), F32),
        vmem((n_bucket, own_r, width), F32),
        vmem((rel_rows, width), F32),
        vmem((2, half_e, width), F32),
        vmem((2, n_rel, own_e, width), F32),
        vmem((own_e, width), F32),
        vmem((ent_rows, width), F32),
        vmem((3, tiles, 1, LANES), jnp.int32),
        vmem((tiles, 1, ent_rows), F32),
        vmem((2, ent_rows, width), BF16),
        vmem((2, rel_rows, width), BF16),
        vmem((2, ent_rows, width), BF16),
        vmem((edges, width), F32),
        vmem((edges, width), F32),
        vmem((edges, width), BF16),
        vmem((edges, width), BF16),
        vmem((edges, ent_rows), F32),
        vmem((ent_rows, edges), BF16),
        vmem((rel_rows, edges), BF16),
        vmem((edges, width), BF16),
        vmem((edges, width), BF16),
        vmem((edges, width), BF16),
        vmem((edges, width), BF16),
        vmem((ent_rows, edges), BF16),
        vmem((ent_rows, edges), BF16),
        vmem((half_r, width), F32),
        vmem((half_r, width), F32),
        vmem((2, ent_rows, width), F32),
        vmem((own_e, width), F32),
        vmem(args[0].shape, F32), vmem(args[1].shape, F32),
        vmem(args[2].shape, F32), vmem(args[3].shape, F32),
        dma((6,)),
        dma, dma,
        dma((2,)), dma((2,)),
        dma((n_bucket,)), dma((n_bucket,)),
        dma((n_bucket,)), dma((n_bucket,)),
        dma((n_bucket,)), dma((n_bucket,)),
        dma((n_bucket,)), dma((n_bucket,)),
        dma((2,)), dma((2,)),
        dma((2, n_rel)), dma((2, n_rel)),
        dma, dma,
        dma((n_rel,)), dma((n_rel,)),
        dma((n_rel,)), dma((n_rel,)),
    ]
    out_shape = tuple(jax.ShapeDtypeStruct(arg.shape, F32) for arg in args[:4])
    made = pl.pallas_call(
        functools.partial(kernel, sizes),
        out_shape=out_shape,
        in_specs=[pl.BlockSpec(memory_space=pltpu.HBM)] * len(args),
        out_specs=[pl.BlockSpec(memory_space=pltpu.HBM)] * 4,
        scratch_shapes=scratch,
        compiler_params=pltpu.CompilerParams(
            collective_id=0, has_side_effects=True, vmem_limit_bytes=60 * 1024 * 1024),
    )(*args)
    new_ent, new_ent_acc, new_rel, new_rel_acc = pl.pallas_call(
        store,
        out_shape=out_shape,
        in_specs=[pl.BlockSpec(memory_space=pltpu.HBM)] * 4,
        out_specs=[pl.BlockSpec(memory_space=pltpu.HBM)] * 4,
        scratch_shapes=[vmem(arg.shape, F32) for arg in args[:4]] + [dma((2, 4))],
        compiler_params=pltpu.CompilerParams(vmem_limit_bytes=60 * 1024 * 1024),
    )(*made)
    return new_ent, new_ent_acc.reshape(-1), new_rel, new_rel_acc.reshape(-1)


def solution(mesh):
    sizes = (mesh.shape["bucket"], mesh.shape["rel"], mesh.shape["sub"])
    edge = P(("groups", "bucket"), "rel", None, None)
    over = P(("groups", "bucket"), "rel", "sub", None, None)
    rows = (
        P(("groups", "bucket"), None),
        P(("groups", "bucket")),
        P(("groups", "rel"), None),
        P(("groups", "rel")),
    )
    return jax.shard_map(
        functools.partial(body, sizes),
        mesh=mesh,
        in_specs=rows + (edge, edge, edge, P(("groups", "bucket"), "rel", None, "sub"),
                         over, over, over, P(("groups", "rel"), "sub", None)),
        out_specs=rows,
        check_vma=False,
    )
```

```python
import functools

import jax
import jax.numpy as jnp
from jax import lax
from jax.experimental import pallas as pl
from jax.experimental.pallas import tpu as pltpu
from jax.sharding import PartitionSpec as P

F32 = jnp.float32
BF16 = jnp.bfloat16
LANES = 128
CHUNK = 256


def mm(a, b):
    return jnp.dot(a, b, preferred_element_type=F32)


def mm_nt(a, b):
    return lax.dot_general(a, b, (((1,), (1,)), ((), ())), preferred_element_type=F32)


def split(x):
    hi = x.astype(BF16)
    return hi, (x - hi.astype(F32)).astype(BF16)


def to_column(row, eye):
    return jnp.sum(jnp.where(eye, row, 0.0), axis=1, keepdims=True)


def to_row(column, eye):
    return jnp.sum(jnp.where(eye, column, 0.0), axis=0, keepdims=True)


def remote(src, dst, send, recv, **target):
    return pltpu.make_async_remote_copy(
        src_ref=src,
        dst_ref=dst,
        send_sem=send,
        recv_sem=recv,
        device_id=target,
        device_id_type=pl.DeviceIdType.MESH,
    )


def kernel(
    sizes,
    a_ent, a_ent_acc, a_rel, a_rel_acc, a_src, a_dst, a_typ, a_neg, a_o_src, a_o_dst, a_o_rel, a_count,
    out_ent, out_ent_acc, out_rel, out_rel_acc,
    ent, ent_acc, rel, rel_acc, e_src, e_dst, e_rel, neg, o_src, o_dst, o_rel, count, s_load,
    neg_in, dst_tab, rel_core, rel_in, rel_all, ent_core, ent_in, moved_in, ent_all,
    ids, weight, src_hl, rel_hl, dst_hl, s_rows, r_rows, q_hi, q_lo, d_hot, s_hot, r_hot,
    xr_hi, xr_lo, xs_hi, xs_lo, gt_hi, gt_lo, rel_out, rel_own, g_ent, share,
    ent_new, ent_new_acc, rel_new, rel_new_acc, s_out,
    s_neg, r_neg, s_tab, r_tab, s_rc, r_rc, s_rz, r_rz, s_ra, r_ra, s_rf, r_rf,
    s_ec, r_ec, s_ex, r_ex, s_mv, r_mv, s_ea, r_ea, s_ef, r_ef,
):
    n_bucket, n_rel, n_sub = sizes
    me_b = lax.axis_index("bucket")
    me_g = lax.axis_index("rel")
    me_s = lax.axis_index("sub")
    other = 1 - me_s
    ent_rows, width = ent.shape
    rel_rows = rel.shape[0]
    half_e, half_r = ent_rows // n_sub, rel_rows // n_sub
    own_e, own_r = half_e // n_rel, half_r // n_bucket
    spill = o_src.shape[0]
    block = e_src.shape[0] // n_sub
    tiles = block + spill
    edges = tiles * LANES

    def around(me, step, n):
        return lax.rem(me + step, n)

    loads = [
        pltpu.make_async_copy(there, here, s_load.at[i])
        for i, (there, here) in enumerate((
            (a_src, e_src), (a_dst, e_dst), (a_typ, e_rel), (a_neg, neg), (a_o_src, o_src),
            (a_o_dst, o_dst), (a_o_rel, o_rel), (a_count, count), (a_ent, ent), (a_rel, rel),
            (a_ent_acc, ent_acc), (a_rel_acc, rel_acc)))
    ]
    for copy in loads:
        copy.start()

    barrier = pltpu.get_barrier_semaphore()
    for k in range(1, n_bucket):
        pl.semaphore_signal(barrier, inc=1, device_id={"bucket": around(me_b, k, n_bucket)},
                            device_id_type=pl.DeviceIdType.MESH)
    for k in range(1, n_rel):
        pl.semaphore_signal(barrier, inc=1, device_id={"rel": around(me_g, k, n_rel)},
                            device_id_type=pl.DeviceIdType.MESH)
    pl.semaphore_signal(barrier, inc=1, device_id={"sub": other},
                        device_id_type=pl.DeviceIdType.MESH)
    pl.semaphore_wait(barrier, n_bucket - 1 + n_rel - 1 + 1)

    my_half = pl.ds(pl.multiple_of(me_s * half_e, half_e), half_e)
    tab = remote(a_ent.at[my_half], dst_tab.at[my_half], s_tab.at[0], r_tab.at[0],
                 bucket=around(me_b, n_bucket - 1, n_bucket))
    tab.start()
    negs = remote(a_neg, neg_in, s_neg, r_neg, sub=other)
    negs.start()

    for copy in loads:
        copy.wait()
    eye = (lax.broadcasted_iota(jnp.int32, (LANES, LANES), 0)
           == lax.broadcasted_iota(jnp.int32, (LANES, LANES), 1))
    lane_e = lax.broadcasted_iota(jnp.int32, (LANES, ent_rows), 1).astype(F32)
    lane_r = lax.broadcasted_iota(jnp.int32, (LANES, rel_rows), 1).astype(F32)
    sub_e = lax.broadcasted_iota(jnp.int32, (ent_rows, LANES), 0)
    sub_r = lax.broadcasted_iota(jnp.int32, (rel_rows, LANES), 0)

    for place, (mine, over) in enumerate(((e_src, o_src), (e_dst, o_dst), (e_rel, o_rel))):
        for t in range(block):
            ids[place, t] = mine[pl.ds(me_s * block + t, 1), :]
        for t in range(spill):
            ids[place, block + t] = over[pl.ds(t, 1), :]

    src_hl[0], src_hl[1] = split(ent[...])
    rel_hl[0], rel_hl[1] = split(rel[...])
    own = jnp.sum(jnp.where(lax.broadcasted_iota(jnp.int32, count.shape, 1) == me_b, count[...], 0)
                  .astype(F32), axis=1, keepdims=True)

    def gather(t, carry):
        rows = pl.ds(pl.multiple_of(t * LANES, LANES), LANES)
        s_id, d_id, r_id = ids[0, t], ids[1, t], ids[2, t]
        hot = (lane_e == to_column(s_id.astype(F32), eye)).astype(F32).astype(BF16)
        s = mm(hot, src_hl[0]) + mm(hot, src_hl[1])
        hot = (lane_r == to_column(r_id.astype(F32), eye)).astype(F32).astype(BF16)
        r = mm(hot, rel_hl[0]) + mm(hot, rel_hl[1])
        s_rows[rows] = s
        r_rows[rows] = r
        q_hi[rows], q_lo[rows] = split(s * r)
        hot = (lane_e == to_column(d_id.astype(F32), eye)).astype(F32)
        d_hot[rows] = hot
        live = ((t - block).astype(F32) < own).astype(F32)
        weight[t] = jnp.sum(hot, axis=0, keepdims=True) * (live * (1.0 / LANES))
        s_hot[:, rows] = (sub_e == s_id).astype(F32).astype(BF16)
        r_hot[:, rows] = (sub_r == r_id).astype(F32).astype(BF16)
        return carry

    lax.fori_loop(0, tiles, gather, 0, unroll=True)

    negs.wait_recv()
    times = jnp.zeros((1, ent_rows), F32)
    for held in (neg, neg_in):
        for t in range(held.shape[0]):
            column = to_column(held[pl.ds(t, 1), :].astype(F32), eye)
            times += jnp.sum((lane_e == column).astype(F32), axis=0, keepdims=True)
    n_neg = n_sub * neg.shape[0] * LANES
    for t in range(block):
        weight[t] = times * (1.0 / n_neg)

    tab.wait_recv()
    tab_core = remote(dst_tab.at[my_half], dst_tab.at[my_half], s_tab.at[1], r_tab.at[1], sub=other)
    tab_core.start()
    tab_core.wait_recv()
    dst_hl[0], dst_hl[1] = split(dst_tab[...])

    def score(c, carry):
        rows = pl.ds(pl.multiple_of(c * CHUNK, CHUNK), CHUNK)
        q_h, q_l = q_hi[rows], q_lo[rows]
        s = mm_nt(q_h, dst_hl[0]) + mm_nt(q_h, dst_hl[1]) + mm_nt(q_l, dst_hl[0])
        sig = lax.logistic(s)
        per = CHUNK // LANES
        w = jnp.concatenate(
            [jnp.broadcast_to(weight[c * per + i], (LANES, ent_rows)) for i in range(per)], axis=0)
        live = jnp.concatenate(
            [jnp.broadcast_to(((c * per + i - block).astype(F32) < own).astype(F32), (LANES, 1))
             for i in range(per)], axis=0)
        g = sig * w + d_hot[rows] * live * (sig - 1.0)
        g_h, g_l = split(g)
        dq = mm(g_h, dst_hl[0]) + mm(g_h, dst_hl[1]) + mm(g_l, dst_hl[0])
        xr_hi[rows], xr_lo[rows] = split(dq * s_rows[rows])
        xs_hi[rows], xs_lo[rows] = split(dq * r_rows[rows])
        gt_hi[:, rows], gt_lo[:, rows] = split(g.T)
        return carry

    lax.fori_loop(0, edges // CHUNK, score, 0, unroll=True)

    mine_r, twin_r = me_s * half_r, other * half_r

    def part(base, k):
        first = base + around(me_b, k % n_bucket, n_bucket) * own_r
        return pl.ds(pl.multiple_of(first, own_r), own_r)

    def scatter_r(base):
        hot = r_hot[pl.ds(pl.multiple_of(base, half_r), half_r), :]
        return mm(hot, xr_hi[...]) + mm(hot, xr_lo[...])

    rel_out[...] = scatter_r(twin_r)
    order = sorted(range(1, n_bucket), key=lambda k: -min(k, n_bucket - k)) + [0]
    rel_c = {}
    for i, k in enumerate(order):
        copy = remote(rel_out.at[part(0, k)], rel_core.at[part(0, k)], s_rc.at[i], r_rc.at[i],
                      sub=other)
        copy.start()
        rel_c[k] = copy

    g_ent[1] = mm(gt_hi[...], q_hi[...]) + mm(gt_hi[...], q_lo[...]) + mm(gt_lo[...], q_hi[...])
    twin_e = pl.ds(pl.multiple_of(other * half_e, half_e), half_e)

    def to_twin(which):
        copy = remote(g_ent.at[which, twin_e], ent_core.at[which], s_ec.at[which], r_ec.at[which],
                      sub=other)
        copy.start()
        return copy

    def to_rel(which):
        copies = []
        for k in range(1, n_rel):
            peer = around(me_g, k, n_rel)
            there = pl.ds(pl.multiple_of(peer * own_e, own_e), own_e)
            copy = remote(ent_core.at[which, there], ent_in.at[which, k], s_ex.at[which, k],
                          r_ex.at[which, k], rel=peer)
            copy.start()
            copies.append(copy)
        return copies

    here_e = pl.ds(pl.multiple_of(me_g * own_e, own_e), own_e)

    def summed(which, copies):
        total = ent_core[which, here_e]
        for k, copy in enumerate(copies):
            copy.wait_recv()
            total = total + ent_in[which, k + 1]
        return total

    dst_c = to_twin(1)

    rel_own[...] = scatter_r(mine_r)

    def of_chip(k):
        rel_c[k].wait_recv()
        rel_core[part(0, k)] = rel_core[part(0, k)] + rel_own[part(0, k)]

    rel_z = []
    for k in order[:-1]:
        of_chip(k)
        slot = k % n_bucket
        copy = remote(rel_core.at[part(0, k)], rel_in.at[slot], s_rz.at[slot], r_rz.at[slot],
                      bucket=around(me_b, slot, n_bucket))
        copy.start()
        rel_z.append((slot, copy))
    of_chip(0)

    dst_c.wait_recv()
    ent_core[1] = ent_core[1] + g_ent[1, my_half]
    dst_x = to_rel(1)
    g_ent[0] = mm(s_hot[...], xs_hi[...]) + mm(s_hot[...], xs_lo[...])
    src_c = to_twin(0)

    src_c.wait_recv()
    ent_core[0] = ent_core[0] + g_ent[0, my_half]
    src_x = to_rel(0)

    share[...] = summed(1, dst_x)
    moved = remote(share, moved_in, s_mv, r_mv, bucket=around(me_b, 1, n_bucket))
    moved.start()

    total = rel_core[part(0, 0)]
    for slot, copy in rel_z:
        copy.wait_recv()
        total = total + rel_in[slot]
    rel_all[part(mine_r, 0)] = total
    rel_a, rel_f = [], []
    for k in order[:-1]:
        slot = k % n_bucket
        copy = remote(rel_all.at[part(mine_r, 0)], rel_all.at[part(mine_r, 0)], s_ra.at[slot],
                      r_ra.at[slot], bucket=around(me_b, slot, n_bucket))
        copy.start()
        rel_a.append((slot, copy))

    def forward_r(rows):
        i = len(rel_f)
        copy = remote(rel_all.at[rows], rel_all.at[rows], s_rf.at[i], r_rf.at[i], sub=other)
        copy.start()
        rel_f.append(copy)

    forward_r(part(mine_r, 0))

    def rows_e(owner):
        return pl.ds(pl.multiple_of(me_s * half_e + owner * own_e, own_e), own_e)

    total = summed(0, src_x)
    moved.wait_recv()
    ent_all[rows_e(me_g)] = total + moved_in[...]
    ent_a, ent_f = [], []
    for k in range(1, n_rel):
        peer = around(me_g, k, n_rel)
        copy = remote(ent_all.at[rows_e(me_g)], ent_all.at[rows_e(me_g)], s_ea.at[k], r_ea.at[k],
                      rel=peer)
        copy.start()
        ent_a.append(copy)

    def forward_e(k):
        there = rows_e(around(me_g, n_rel - k, n_rel))
        copy = remote(ent_all.at[there], ent_all.at[there], s_ef.at[k], r_ef.at[k], sub=other)
        copy.start()
        ent_f.append(copy)

    forward_e(0)

    for slot, copy in reversed(rel_a):
        copy.wait_recv()
        forward_r(part(mine_r, -slot))

    stores = []

    def adagrad(table, accum, grads, staged, staged_acc, out, first, count, sem):
        first = pl.multiple_of(first, count)
        for i in range(count // LANES):
            rows = pl.ds(pl.multiple_of(first + i * LANES, LANES), LANES)
            at = pl.ds(first // LANES + i, 1)
            grad = grads[rows]
            fresh = (to_column(accum[at, :], eye)
                     + jnp.sum(grad * grad, axis=1, keepdims=True) * (1.0 / width))
            staged[rows] = table[rows] - grad * (0.1 * lax.rsqrt(fresh))
            staged_acc[at, :] = to_row(fresh, eye)
        whole = pl.ds(first, count)
        copy = pltpu.make_async_copy(staged.at[whole], out.at[whole], s_out.at[sem])
        copy.start()
        stores.append(copy)

    adagrad(rel, rel_acc, rel_all, rel_new, rel_new_acc, out_rel, mine_r, half_r, 0)
    for k in range(1, n_rel):
        ent_a[k - 1].wait_recv()
        forward_e(k)
    adagrad(ent, ent_acc, ent_all, ent_new, ent_new_acc, out_ent, me_s * half_e, half_e, 1)
    for copy in rel_f:
        copy.wait_recv()
    adagrad(rel, rel_acc, rel_all, rel_new, rel_new_acc, out_rel, twin_r, half_r, 2)
    for copy in ent_f:
        copy.wait_recv()
    adagrad(ent, ent_acc, ent_all, ent_new, ent_new_acc, out_ent, other * half_e, half_e, 3)
    for i, (here, there) in enumerate(((rel_new_acc, out_rel_acc), (ent_new_acc, out_ent_acc))):
        copy = pltpu.make_async_copy(here, there, s_out.at[4 + i])
        copy.start()
        stores.append(copy)

    for copy in [tab, negs, tab_core, dst_c, src_c, moved] + (
            list(rel_c.values()) + [copy for _, copy in rel_z + rel_a]
            + dst_x + src_x + rel_f + ent_a + ent_f):
        copy.wait_send()
    for copy in stores:
        copy.wait()


def store(*refs):
    made, out, held, sems = refs[:4], refs[4:8], refs[8:12], refs[12]
    loads = [pltpu.make_async_copy(made[i], held[i], sems.at[0, i]) for i in range(4)]
    stores = [pltpu.make_async_copy(held[i], out[i], sems.at[1, i]) for i in range(4)]
    for load in loads:
        load.start()
    for load, copy in zip(loads, stores):
        load.wait()
        copy.start()
    for copy in stores:
        copy.wait()


def body(sizes, entity, entity_acc, relation, relation_acc, edge_src, edge_dst, edge_rel, negatives,
         ovf_src, ovf_dst, ovf_rel, ovf_count):
    n_bucket, n_rel, n_sub = sizes
    ent_rows, width = entity.shape
    rel_rows = relation.shape[0]
    lined = lambda x: x.reshape(-1, LANES)
    half_e, half_r = ent_rows // n_sub, rel_rows // n_sub
    own_e, own_r = half_e // n_rel, half_r // n_bucket
    tiles = edge_src.size // n_sub // LANES + ovf_src.size // LANES
    edges = tiles * LANES
    neg_rows = negatives.size // LANES
    vmem = pltpu.VMEM
    dma = pltpu.SemaphoreType.DMA
    args = (
        entity, lined(entity_acc), relation, lined(relation_acc),
        lined(edge_src), lined(edge_dst), lined(edge_rel), lined(negatives),
        lined(ovf_src), lined(ovf_dst), lined(ovf_rel), ovf_count.reshape(1, -1),
    )
    scratch = [vmem(arg.shape, arg.dtype) for arg in args] + [dma((len(args),))] + [
        vmem((neg_rows, LANES), jnp.int32),
        vmem((ent_rows, width), F32),
        vmem((half_r, width), F32),
        vmem((n_bucket, own_r, width), F32),
        vmem((rel_rows, width), F32),
        vmem((2, half_e, width), F32),
        vmem((2, n_rel, own_e, width), F32),
        vmem((own_e, width), F32),
        vmem((ent_rows, width), F32),
        vmem((3, tiles, 1, LANES), jnp.int32),
        vmem((tiles, 1, ent_rows), F32),
        vmem((2, ent_rows, width), BF16),
        vmem((2, rel_rows, width), BF16),
        vmem((2, ent_rows, width), BF16),
        vmem((edges, width), F32),
        vmem((edges, width), F32),
        vmem((edges, width), BF16),
        vmem((edges, width), BF16),
        vmem((edges, ent_rows), F32),
        vmem((ent_rows, edges), BF16),
        vmem((rel_rows, edges), BF16),
        vmem((edges, width), BF16),
        vmem((edges, width), BF16),
        vmem((edges, width), BF16),
        vmem((edges, width), BF16),
        vmem((ent_rows, edges), BF16),
        vmem((ent_rows, edges), BF16),
        vmem((half_r, width), F32),
        vmem((half_r, width), F32),
        vmem((2, ent_rows, width), F32),
        vmem((own_e, width), F32),
        vmem(args[0].shape, F32), vmem(args[1].shape, F32),
        vmem(args[2].shape, F32), vmem(args[3].shape, F32),
        dma((6,)),
        dma, dma,
        dma((2,)), dma((2,)),
        dma((n_bucket,)), dma((n_bucket,)),
        dma((n_bucket,)), dma((n_bucket,)),
        dma((n_bucket,)), dma((n_bucket,)),
        dma((n_bucket,)), dma((n_bucket,)),
        dma((2,)), dma((2,)),
        dma((2, n_rel)), dma((2, n_rel)),
        dma, dma,
        dma((n_rel,)), dma((n_rel,)),
        dma((n_rel,)), dma((n_rel,)),
    ]
    out_shape = tuple(jax.ShapeDtypeStruct(arg.shape, F32) for arg in args[:4])
    made = pl.pallas_call(
        functools.partial(kernel, sizes),
        out_shape=out_shape,
        in_specs=[pl.BlockSpec(memory_space=pltpu.HBM)] * len(args),
        out_specs=[pl.BlockSpec(memory_space=pltpu.HBM)] * 4,
        scratch_shapes=scratch,
        compiler_params=pltpu.CompilerParams(
            collective_id=0, has_side_effects=True, vmem_limit_bytes=60 * 1024 * 1024),
    )(*args)
    new_ent, new_ent_acc, new_rel, new_rel_acc = pl.pallas_call(
        store,
        out_shape=out_shape,
        in_specs=[pl.BlockSpec(memory_space=pltpu.HBM)] * 4,
        out_specs=[pl.BlockSpec(memory_space=pltpu.HBM)] * 4,
        scratch_shapes=[vmem(arg.shape, F32) for arg in args[:4]] + [dma((2, 4))],
        compiler_params=pltpu.CompilerParams(vmem_limit_bytes=60 * 1024 * 1024),
    )(*made)
    return new_ent, new_ent_acc.reshape(-1), new_rel, new_rel_acc.reshape(-1)


def solution(mesh):
    sizes = (mesh.shape["bucket"], mesh.shape["rel"], mesh.shape["sub"])
    edge = P(("groups", "bucket"), "rel", None, None)
    over = P(("groups", "bucket"), "rel", "sub", None, None)
    rows = (
        P(("groups", "bucket"), None),
        P(("groups", "bucket")),
        P(("groups", "rel"), None),
        P(("groups", "rel")),
    )
    return jax.shard_map(
        functools.partial(body, sizes),
        mesh=mesh,
        in_specs=rows + (edge, edge, edge, P(("groups", "bucket"), "rel", None, "sub"),
                         over, over, over, P(("groups", "rel"), "sub", None)),
        out_specs=rows,
        check_vma=False,
    )
```
